256 devices in a mesh: tm: 16 (over z, core), chan: 8 (over x_hi, y), hank: 2 (over x_lo).
Axes of the slice: x: 4 (x_hi: 2, x_lo: 2; x = x_hi * 2 + x_lo), y: 4, z: 8, core: 2. Of those that a mesh axis runs over, the one named last changes fastest.
Arguments:
- records: bfloat16 [8192, 8192], P('tm', 'chan'), may hold values from -6 to 6
- ref_blocks: int32 [16], replicated, may hold values from 0 to 63, as said below
- probe_seed: int32 [1], replicated, may hold values from 0 to 1048575
Outputs:
- range_sketch: float32 [8, 1024, 16, 512], P('chan', 'tm', 'hank')
The draws below stay inside these ranges and needn't reach their ends.
Inputs may be any that keep to these rules, and one draw needn't show every extreme that they name: `ref_blocks`: distinct channel block numbers; the first and the last block of the channels are always among them.
All inputs are finite; a program needn't handle non-finite values.
Results may differ from the reference program's by a relative error of at most 0.0029.
Values may be sent and summed in bfloat16 or wider, within the bound.
No kernel may reach another device: no remote copies, remote signals or barrier semaphores. Data moves between devices by JAX's collectives and lax.ppermute only.
A program may use at most 128 MiB of HBM per device.

```python
import math
import jax
import jax.numpy as jnp
from jax import lax

CH_DEV = 1024
REF = 2048
BLK = 128
Q = 16
P_SIZE = 512
TIME = 8192
CH = 8192
N_CHAN = 8


def draw_ref_blocks(key, part):
    block_total = CH // BLK
    chosen_count = REF // BLK
    first_key = jax.random.fold_in(key, 11)
    second_key = jax.random.fold_in(key, 23)
    inner = jax.random.permutation(first_key, block_total - 2)[:chosen_count - 2].astype(jnp.int32) + 1
    chosen = jnp.concatenate([jnp.array([0, block_total - 1], dtype=jnp.int32), inner])
    order = jax.random.permutation(second_key, chosen_count)
    return chosen[order].astype(jnp.int32)


def strengthened(values, rng, source, target, blocks, factor):
    def block_of(axis_at):
        return (jnp.arange(values.shape[axis_at]) // (values.shape[axis_at] // blocks)).reshape((-1,) + (1,) * (values.ndim - 1 - axis_at))

    near = jax.random.permutation(rng, blocks)[block_of(target)]
    other_side = (block_of(target) + blocks // 2) % blocks
    return jnp.where((block_of(source) == near) | (block_of(source) == other_side), factor * values, values)


def steps_of(stream_key, extent, split, low, top_value):
    def one(axis_at, parts):
        heights = jax.random.uniform(jax.random.fold_in(jax.random.fold_in(stream_key, 6), axis_at), (parts,), jnp.float32, low / len(split), top_value / len(split))
        return jnp.repeat(jnp.exp(heights), extent[axis_at] // parts).reshape((-1,) + (1,) * (len(extent) - axis_at - 1))

    level = one(*split[0])
    for cut in split[1:]:
        level = level * one(*cut)
    return level


def heavy_noise(stream_key, shape, scale, bound, cuts, heavy, kind=jnp.bfloat16):
    values = scale * jax.random.normal(stream_key, shape, jnp.float32)
    if cuts:
        values = values * steps_of(stream_key, shape, cuts, -0.22, 0.18)
    return jnp.clip(strengthened(values, jax.random.fold_in(stream_key, 3), *heavy), -bound, bound).astype(kind)


def setup_inputs(seed: int = 0) -> dict:
    splits = jax.random.split(jax.random.key(seed), 4)
    records = heavy_noise(splits[0], (TIME, CH), 1.0, 6.0, ((0, 16), (1, 8)), (0, 1, 16, 2.0))
    ref_blocks = draw_ref_blocks(jax.random.fold_in(splits[3], 71), 0)
    probe_seed = jax.random.randint(splits[2], (1,), 0, 1048576).astype(jnp.int32)
    return {"records": records, "ref_blocks": ref_blocks, "probe_seed": probe_seed}


def probe_table(probe_seed, j_first, j_count, r_first, r_count):
    j_ids = (j_first + jnp.arange(j_count, dtype=jnp.int32))[:, None, None]
    r_ids = (r_first + jnp.arange(r_count, dtype=jnp.int32))[None, :, None]
    p_ids = jnp.arange(P_SIZE, dtype=jnp.int32)[None, None, :]
    flat_index = (j_ids * REF + r_ids) * P_SIZE + p_ids
    mixed = flat_index + probe_seed[0] * 7919
    mixed = mixed ^ mixed >> 15
    mixed = mixed * 668265263
    mixed = mixed ^ mixed >> 13
    low_bit = mixed >> 9 & 1
    return (1 - 2 * low_bit).astype(jnp.float32).astype(jnp.bfloat16)

def reference(records, ref_blocks, probe_seed):
    total_time = records.shape[0]
    blocks = records.reshape(total_time, CH // BLK, BLK)
    ref_records = jnp.take(blocks, ref_blocks, axis=1).reshape(total_time, REF)
    probes = probe_table(probe_seed, 0, Q, 0, REF)
    padded = jnp.concatenate([jnp.zeros((Q, REF), jnp.bfloat16), ref_records], axis=0)

    def add_lag(running, lag_step):
        segment = lax.dynamic_slice_in_dim(padded, (Q - lag_step).astype(jnp.int32), total_time, 0)
        return (running + jnp.dot(segment, probes[lag_step], preferred_element_type=jnp.float32), None)
    images, _ = lax.scan(add_lag, jnp.zeros((total_time, P_SIZE), jnp.float32), jnp.arange(Q, dtype=jnp.int32))
    images = images.astype(jnp.bfloat16)
    ahead = jnp.concatenate([records, jnp.zeros((Q + 1, CH), jnp.bfloat16)], axis=0)

    def block_row(row_index):
        segment = lax.dynamic_slice_in_dim(ahead, (row_index + 1).astype(jnp.int32), total_time, 0)
        return jnp.dot(segment.T, images, preferred_element_type=jnp.float32)
    sketch = lax.map(block_row, jnp.arange(Q, dtype=jnp.int32))
    factor = 1.0 / math.sqrt(total_time * Q * REF)
    sketch = sketch * factor
    return sketch.reshape(Q, N_CHAN, CH_DEV, P_SIZE).transpose(1, 2, 0, 3)
```

```python
import functools
import math

import jax
import jax.numpy as jnp
from jax import lax
from jax.experimental import pallas as pl
from jax.experimental.pallas import tpu as pltpu
from jax.sharding import PartitionSpec as P

REF = 2048
BLK = 128
Q = 16
P_SIZE = 512
HALF_P = P_SIZE // 2
LAGS = Q // 2
ROWS = 512
NZ = 8
NCHAN = 8
CDEV = 64
F32 = jnp.float32
BF16 = jnp.bfloat16
VMEM = pltpu.VMEM
SMEM = pltpu.SMEM


def tm_shift(value, steps):
    first, last = max(0, -steps), min(16, 16 - steps)
    return lax.ppermute(value, "tm", [(i, i + steps) for i in range(first, last)])


def z_shift(value, steps):
    return lax.ppermute(value, "tm", [(i, (i + 2 * steps) % 16) for i in range(16)])


def core_swap(value):
    return lax.ppermute(value, "tm", [(i, i ^ 1) for i in range(16)])


def hank_swap(value):
    return lax.ppermute(value, "hank", [(0, 1), (1, 0)])


def chan_xor(value, bit):
    return lax.ppermute(value, "chan", [(i, i ^ bit) for i in range(NCHAN)])


def images_kernel(place, blocks, seed, records, behind, out, staged, shifted, signs):
    first_block = place[0] * (1024 // BLK)
    start = seed[0] * 7919 + place[1] * HALF_P
    out[...] = jnp.zeros_like(out)

    def step(q, carry):
        local = blocks[q] - first_block

        @pl.when((local >= 0) & (local < 1024 // BLK))
        def _():
            cols = pl.ds(pl.multiple_of(local * BLK, BLK), BLK)
            staged[pl.ds(0, Q), :] = behind[:, cols].astype(F32)
            staged[pl.ds(Q, ROWS), :] = records[:, cols].astype(F32)
            index = lax.broadcasted_iota(jnp.int32, (BLK, HALF_P), 0) * P_SIZE
            index = index + lax.broadcasted_iota(jnp.int32, (BLK, HALF_P), 1)
            for j in range(Q):
                shifted[:, j * BLK : (j + 1) * BLK] = staged[pl.ds(Q - j, ROWS), :].astype(BF16)
                mixed = index + (start + (j * REF + q * BLK) * P_SIZE)
                mixed = mixed ^ (mixed >> 15)
                mixed = mixed * 668265263
                mixed = mixed ^ (mixed >> 13)
                sign = jnp.where((mixed & 512) != 0, F32(-1), F32(1))
                signs[j * BLK : (j + 1) * BLK, :] = sign.astype(BF16)
            out[...] += jnp.dot(shifted[...], signs[...], preferred_element_type=F32)

        return carry

    lax.fori_loop(0, REF // BLK, step, 0)


def partial_images(place, ref_blocks, probe_seed, records, behind):
    return pl.pallas_call(
        images_kernel,
        out_shape=jax.ShapeDtypeStruct((ROWS, HALF_P), F32),
        in_specs=[pl.BlockSpec(memory_space=SMEM)] * 3 + [pl.BlockSpec(memory_space=VMEM)] * 2,
        out_specs=pl.BlockSpec(memory_space=VMEM),
        scratch_shapes=[
            pltpu.VMEM((ROWS + Q, BLK), F32),
            pltpu.VMEM((ROWS, Q * BLK), BF16),
            pltpu.VMEM((Q * BLK, HALF_P), BF16),
        ],
        compiler_params=pltpu.CompilerParams(vmem_limit_bytes=24 << 20),
        cost_estimate=pl.CostEstimate(flops=3 << 30, bytes_accessed=2 << 20, transcendentals=0),
        name="partial_images",
    )(place, ref_blocks, probe_seed, records, behind)


def lagged_kernel(place, rows, ahead, out, wide):
    wide[pl.ds(0, ROWS), :] = rows[0].astype(F32)
    wide[pl.ds(ROWS, Q), :] = ahead[0].astype(F32)
    wide[pl.ds(ROWS + Q, BLK - Q), :] = jnp.zeros((BLK - Q, BLK), F32)
    turned = pltpu.roll(wide[...], place[2] * CDEV, 1).T
    span = ROWS + BLK
    for side in range(2):
        half = place[1] if side == 0 else 1 - place[1]
        first = pltpu.roll(turned, (span - half * LAGS) % span, 1)
        for i in range(LAGS):
            moved = pltpu.roll(first, span - (i + 1), 1)[:, :ROWS].astype(BF16)
            for other in range(2):
                at = ((other * 2 + side) * LAGS + i) * CDEV
                out[0, pl.ds(at, CDEV), :] = moved[other * CDEV : (other + 1) * CDEV]


def lagged_records(place, rows, ahead):
    return pl.pallas_call(
        lagged_kernel,
        grid=(NZ,),
        out_shape=jax.ShapeDtypeStruct((NZ, 2 * Q * CDEV, ROWS), BF16),
        in_specs=[
            pl.BlockSpec(memory_space=SMEM),
            pl.BlockSpec((1, ROWS, BLK), lambda k: (k, 0, 0)),
            pl.BlockSpec((1, Q, BLK), lambda k: (k, 0, 0)),
        ],
        out_specs=pl.BlockSpec((1, 2 * Q * CDEV, ROWS), lambda k: (k, 0, 0)),
        scratch_shapes=[pltpu.VMEM((ROWS + BLK, BLK), F32)],
        compiler_params=pltpu.CompilerParams(vmem_limit_bytes=24 << 20),
        cost_estimate=pl.CostEstimate(flops=1 << 28, bytes_accessed=18 << 20, transcendentals=0),
        name="lagged_records",
    )(place, rows, ahead)


def sketch_kernel(count, first, *refs):
    lagged, images = refs[:count], refs[count : 2 * count]
    out = refs[-1]
    total = None
    for left, right in zip(lagged, images):
        term = jnp.dot(left[0], right[...], preferred_element_type=F32)
        total = term if total is None else total + term
    if not first:
        total = total + refs[2 * count][...]
    out[...] = total


def sketch_terms(lagged, pieces, running):
    block = 512
    count = len(pieces)
    places = [k for k, _ in pieces]
    in_specs = [pl.BlockSpec((1, block, ROWS), lambda m, k=k: (k, m, 0)) for k in places]
    in_specs += [pl.BlockSpec((ROWS, HALF_P), lambda m: (0, 0))] * count
    args = [lagged] * count + [image for _, image in pieces]
    aliases = {}
    if running is not None:
        in_specs.append(pl.BlockSpec((block, HALF_P), lambda m: (m, 0)))
        args.append(running)
        aliases = {2 * count: 0}
    return pl.pallas_call(
        functools.partial(sketch_kernel, count, running is None),
        grid=(2 * Q * CDEV // block,),
        out_shape=jax.ShapeDtypeStruct((2 * Q * CDEV, HALF_P), F32),
        in_specs=in_specs,
        out_specs=pl.BlockSpec((block, HALF_P), lambda m: (m, 0)),
        input_output_aliases=aliases,
        compiler_params=pltpu.CompilerParams(vmem_limit_bytes=24 << 20),
        cost_estimate=pl.CostEstimate(flops=count << 29, bytes_accessed=(2 * count + 4) << 20, transcendentals=0),
        name="sketch_terms",
    )(*args)


def final_kernel(factor, place, own, near, far, out):
    mine = pl.ds(pl.multiple_of(place[1] * HALF_P, HALF_P), HALF_P)
    theirs = pl.ds(pl.multiple_of((1 - place[1]) * HALF_P, HALF_P), HALF_P)
    for i in range(LAGS):
        out[:, i, mine] = (own[i] + near[i]) * factor
        out[:, i, theirs] = far[i].astype(F32) * factor


def final_sketch(factor, place, own, near, far):
    return pl.pallas_call(
        functools.partial(final_kernel, factor),
        out_shape=jax.ShapeDtypeStruct((CDEV, LAGS, P_SIZE), F32),
        in_specs=[pl.BlockSpec(memory_space=SMEM)] + [pl.BlockSpec(memory_space=VMEM)] * 3,
        out_specs=pl.BlockSpec(memory_space=VMEM),
        compiler_params=pltpu.CompilerParams(vmem_limit_bytes=16 << 20),
        name="final_sketch",
    )(place, own, near, far)


def per_device(records, ref_blocks, probe_seed):
    tm = lax.axis_index("tm")
    z, core = tm // 2, tm % 2
    hank = lax.axis_index("hank")
    chan = lax.axis_index("chan")
    place = jnp.stack([chan, hank, core]).astype(jnp.int32)

    behind = tm_shift(records[ROWS - Q :], 1)
    rows = []
    for k in range(NZ):
        target = (z + k) % NZ
        piece = lax.dynamic_slice_in_dim(records, target * BLK, BLK, 1)
        rows.append(piece if k == 0 else z_shift(piece, k))
    rows = jnp.stack(rows)

    partial = partial_images(place, ref_blocks, probe_seed, records, behind)
    parts = lax.all_to_all(partial.reshape(NCHAN, ROWS // NCHAN, HALF_P), "chan", 0, 0, tiled=True)
    image = jnp.sum(parts, axis=0).astype(BF16)

    fronts = rows[:, :Q]
    given = core_swap(fronts)
    later = jnp.concatenate([given[NZ - 1 :], given[: NZ - 1]], axis=0)
    last_block = ((z - jnp.arange(NZ)) % NZ == NZ - 1)[:, None, None]
    later = jnp.where(last_block, jnp.zeros_like(later), later)
    ahead = jnp.where(core == 0, given, later)
    lagged = lagged_records(place, rows, ahead)

    for bit in (1, 2, 4):
        other = chan_xor(image, bit)
        upper = (chan & bit) != 0
        image = jnp.concatenate([jnp.where(upper, other, image), jnp.where(upper, image, other)], axis=0)

    running = None
    forward = backward = image
    arrived = [(0, image)]
    for step in range(1, 5):
        forward = z_shift(forward, 1)
        nxt = [(step, forward)]
        if step < 4:
            backward = z_shift(backward, -1)
            nxt.append((NZ - step, backward))
        running = sketch_terms(lagged, arrived, running)
        arrived = nxt
    running = sketch_terms(lagged, arrived, running)

    total = running.reshape(2, 2, LAGS, CDEV, HALF_P)
    near_far = core_swap(total[1, 1])
    far = hank_swap((total[0, 1] + near_far).astype(BF16))
    near = core_swap(total[1, 0])
    factor = 1.0 / math.sqrt(ROWS * 16 * Q * REF)
    return final_sketch(factor, place, total[0, 0], near, far)[None]


def solution(mesh):
    in_specs = (P("tm", "chan"), P(), P())
    out_specs = P("chan", "tm", "hank", None)
    return jax.shard_map(
        per_device, mesh=mesh, in_specs=in_specs, out_specs=out_specs, check_vma=False
    )
```

```python
import functools
import math

import jax
import jax.numpy as jnp
from jax import lax
from jax.experimental import pallas as pl
from jax.experimental.pallas import tpu as pltpu
from jax.sharding import PartitionSpec as P

REF = 2048
BLK = 128
Q = 16
P_SIZE = 512
HALF_P = P_SIZE // 2
LAGS = Q // 2
ROWS = 512
NZ = 8
NCHAN = 8
CDEV = 64
SHARE = ROWS // NCHAN
F32 = jnp.float32
BF16 = jnp.bfloat16
VMEM = pltpu.VMEM
SMEM = pltpu.SMEM


def tm_shift(value, steps):
    first, last = max(0, -steps), min(16, 16 - steps)
    return lax.ppermute(value, "tm", [(i, i + steps) for i in range(first, last)])


def z_shift(value, steps):
    return lax.ppermute(value, "tm", [(i, (i + 2 * steps) % 16) for i in range(16)])


def split_shift(value, near, far):
    pairs = []
    for i in range(16):
        pairs.append((2 * i, 2 * ((i + 2 * near) % 16)))
        pairs.append((2 * i + 1, 2 * ((i + 2 * far) % 16) + 1))
    return lax.ppermute(value, ("tm", "hank"), pairs)


def core_swap(value):
    return lax.ppermute(value, "tm", [(i, i ^ 1) for i in range(16)])


def hank_swap(value):
    return lax.ppermute(value, "hank", [(0, 1), (1, 0)])


def y_shift(value, steps):
    return lax.ppermute(value, "chan", [(i, (i & 4) | ((i + steps) & 3)) for i in range(NCHAN)])


def x_swap(value):
    return lax.ppermute(value, "chan", [(i, i ^ 4) for i in range(NCHAN)])


def signs_kernel(place, blocks, seed, signs):
    first_block = place[0] * (1024 // BLK)
    start = seed[0] * 7919 + place[1] * HALF_P

    def step(q, used):
        local = blocks[q] - first_block
        owned = (local >= 0) & (local < 1024 // BLK)

        @pl.when(owned)
        def _():
            index = lax.broadcasted_iota(jnp.int32, (BLK, HALF_P), 0) * P_SIZE
            index = index + lax.broadcasted_iota(jnp.int32, (BLK, HALF_P), 1)
            for j in range(Q):
                mixed = index + (start + (j * REF + q * BLK) * P_SIZE)
                mixed = mixed ^ (mixed >> 15)
                mixed = mixed * 668265263
                mixed = mixed ^ (mixed >> 13)
                sign = jnp.where((mixed & 512) != 0, F32(-1), F32(1))
                signs[used, j * BLK : (j + 1) * BLK, :] = sign.astype(BF16)

        return used + owned.astype(jnp.int32)

    lax.fori_loop(0, REF // BLK, step, jnp.int32(0))


def images_kernel(place, blocks, records, behind, signs, out, staged, shifted):
    first_block = place[0] * (1024 // BLK)
    out[...] = jnp.zeros_like(out)

    def step(q, used):
        local = blocks[q] - first_block
        owned = (local >= 0) & (local < 1024 // BLK)

        @pl.when(owned)
        def _():
            cols = pl.ds(pl.multiple_of(local * BLK, BLK), BLK)
            staged[pl.ds(0, Q), :] = behind[:, cols].astype(F32)
            staged[pl.ds(Q, ROWS), :] = records[:, cols].astype(F32)
            for j in range(Q):
                shifted[:, j * BLK : (j + 1) * BLK] = staged[pl.ds(Q - j, ROWS), :].astype(BF16)
            out[...] += jnp.dot(shifted[...], signs[used], preferred_element_type=F32)

        return used + owned.astype(jnp.int32)

    lax.fori_loop(0, REF // BLK, step, jnp.int32(0))


def probe_signs(place, ref_blocks, probe_seed):
    return pl.pallas_call(
        signs_kernel,
        out_shape=jax.ShapeDtypeStruct((1024 // BLK, Q * BLK, HALF_P), BF16),
        in_specs=[pl.BlockSpec(memory_space=SMEM)] * 3,
        out_specs=pl.BlockSpec(memory_space=VMEM),
        compiler_params=pltpu.CompilerParams(vmem_limit_bytes=16 << 20),
        cost_estimate=pl.CostEstimate(flops=0, bytes_accessed=14 << 20, transcendentals=0),
        name="probe_signs",
    )(place, ref_blocks, probe_seed)


def partial_images(place, ref_blocks, records, behind, signs):
    return pl.pallas_call(
        images_kernel,
        out_shape=jax.ShapeDtypeStruct((ROWS, HALF_P), F32),
        in_specs=[pl.BlockSpec(memory_space=SMEM)] * 2 + [pl.BlockSpec(memory_space=VMEM)] * 3,
        out_specs=pl.BlockSpec(memory_space=VMEM),
        scratch_shapes=[pltpu.VMEM((ROWS + Q, BLK), F32), pltpu.VMEM((ROWS, Q * BLK), BF16)],
        compiler_params=pltpu.CompilerParams(vmem_limit_bytes=24 << 20),
        cost_estimate=pl.CostEstimate(flops=4 << 30, bytes_accessed=2 << 20, transcendentals=0),
        name="partial_images",
    )(place, ref_blocks, records, behind, signs)


def order_kernel(place, *refs):
    out, staged = refs[-2:]
    at = 0
    for ref in refs[:-2]:
        for entry in range(ref.shape[0]):
            k = ((place[0] & 4) ^ (at & 4)) | ((place[0] - at) & 3)
            staged[pl.ds(pl.multiple_of(k * SHARE, SHARE), SHARE), :] = ref[entry].astype(F32)
            at += 1
    out[...] = staged[...].T.astype(BF16)


def turned_image(place, parts):
    return pl.pallas_call(
        order_kernel,
        out_shape=jax.ShapeDtypeStruct((HALF_P, ROWS), BF16),
        in_specs=[pl.BlockSpec(memory_space=SMEM)] + [pl.BlockSpec(memory_space=VMEM)] * len(parts),
        out_specs=pl.BlockSpec(memory_space=VMEM),
        scratch_shapes=[pltpu.VMEM((ROWS, HALF_P), F32)],
        compiler_params=pltpu.CompilerParams(vmem_limit_bytes=8 << 20),
        cost_estimate=pl.CostEstimate(flops=0, bytes_accessed=3 << 20, transcendentals=0),
        name="turned_image",
    )(place, *parts)


def sketch_kernel(count, starts, turn, first, last, *refs):
    place, ahead = refs[:2]
    inputs = len(starts)
    rows, images = refs[2 : 2 + inputs], refs[2 + inputs : 2 + inputs + count]
    staged, total = refs[-2:]
    out = refs[-3]
    running = None if first else refs[2 + inputs + count]
    for n in range(count):
        if inputs == count:
            staged[pl.ds(0, ROWS), :] = rows[n][pl.ds(starts[n], ROWS), :].astype(F32)
        else:
            for m in range(2):
                at = pl.multiple_of((place[1] ^ m) * (ROWS // 2), ROWS // 2)
                staged[pl.ds(at, ROWS // 2), :] = rows[m][pl.ds(starts[m], ROWS // 2), :].astype(F32)
        staged[pl.ds(ROWS, Q), :] = ahead[n].astype(F32)
        image = images[n][...]
        if count == 2:
            image = jnp.where(place[1] == turn, image, images[1 - n][...])
        for m in range(LAGS):
            pair = [staged[pl.ds(2 * m + 1 + i, ROWS), :].astype(BF16) for i in range(2)]
            term = jnp.dot(image, jnp.concatenate(pair, axis=1), preferred_element_type=F32)
            at = slice(2 * m * BLK, (2 * m + 2) * BLK)
            goal = total if last or n < count - 1 else out
            if n == 0:
                goal[:, at] = term if first else running[:, at] + term
            else:
                goal[:, at] = total[:, at] + term
    if last:
        lane = lax.broadcasted_iota(jnp.int32, (HALF_P, BLK), 1)
        for m in range(LAGS):
            even = total[:, 2 * m * BLK : (2 * m + 1) * BLK]
            odd = total[:, (2 * m + 1) * BLK : (2 * m + 2) * BLK]
            low = jnp.where(lane < CDEV, even, pltpu.roll(odd, CDEV, 1))
            high = jnp.where(lane < CDEV, pltpu.roll(even, CDEV, 1), odd)
            side = (m // 4) ^ place[1]
            out[place[2], side, m % 4] = low
            out[1 - place[2], side, m % 4] = high


def sketch_terms(place, ahead, rows, images, turn, running, last=False):
    count, first = len(images), running is None
    starts = [start for _, start in rows]
    rows = [value for value, _ in rows]
    shape = (2, 2, 4, HALF_P, BLK) if last else (HALF_P, Q * BLK)
    args = [place, ahead, *rows, *images] + ([] if first else [running])
    return pl.pallas_call(
        functools.partial(sketch_kernel, count, starts, turn, first, last),
        out_shape=jax.ShapeDtypeStruct(shape, F32),
        in_specs=[pl.BlockSpec(memory_space=SMEM)] + [pl.BlockSpec(memory_space=VMEM)] * (len(args) - 1),
        out_specs=pl.BlockSpec(memory_space=VMEM),
        scratch_shapes=[pltpu.VMEM((ROWS + Q, BLK), F32), pltpu.VMEM((HALF_P, Q * BLK), F32)],
        compiler_params=pltpu.CompilerParams(vmem_limit_bytes=24 << 20),
        cost_estimate=pl.CostEstimate(flops=count << 30, bytes_accessed=2 << 20, transcendentals=0),
        name="sketch_terms",
    )(*args)


def final_kernel(factor, count, place, *refs):
    out = refs[-1]
    for m in range(LAGS // 2):
        value = refs[0][m].astype(F32)
        if count == 2:
            value = value + refs[1][m]
        value = (value * factor).T
        for i in range(2):
            out[:, 2 * m + i, :] = value[i * CDEV : (i + 1) * CDEV]


def final_sketch(factor, place, side, terms, out):
    whole = pl.BlockSpec((LAGS // 2, HALF_P, BLK), lambda i, place: (0, 0, 0))
    goal = pl.BlockSpec((CDEV, LAGS, HALF_P), lambda i, place: (0, 0, place[1] ^ side))
    args = list(terms)
    in_specs = [whole] * len(terms)
    aliases = {}
    if out is not None:
        args.append(out)
        in_specs.append(pl.BlockSpec(memory_space=pl.ANY))
        aliases = {len(terms) + 1: 0}
    return pl.pallas_call(
        functools.partial(final_kernel, factor, len(terms)),
        out_shape=jax.ShapeDtypeStruct((CDEV, LAGS, P_SIZE), F32),
        grid_spec=pltpu.PrefetchScalarGridSpec(
            num_scalar_prefetch=1, grid=(1,), in_specs=in_specs, out_specs=goal
        ),
        input_output_aliases=aliases,
        compiler_params=pltpu.CompilerParams(vmem_limit_bytes=16 << 20),
        name="final_sketch",
    )(place, *args)


def per_device(records, ref_blocks, probe_seed):
    tm = lax.axis_index("tm")
    z, core = tm >> 1, tm & 1
    hank = lax.axis_index("hank")
    chan = lax.axis_index("chan")
    place = jnp.stack([chan, hank, core]).astype(jnp.int32)

    behind = tm_shift(records[ROWS - Q :], 1)
    signs = probe_signs(place, ref_blocks, probe_seed)
    partial = partial_images(place, ref_blocks, records, behind, signs)

    partial, sent = lax.optimization_barrier((partial, records))
    parts = lax.all_to_all(partial.reshape(NCHAN, SHARE, HALF_P), "chan", 0, 0, tiled=True)
    sign = 1 - 2 * hank

    def piece(steps):
        return lax.dynamic_slice_in_dim(sent, ((z + steps) & (NZ - 1)) * BLK, BLK, 1)

    own = piece(0)
    half = lax.dynamic_slice_in_dim(piece(4), hank * (ROWS // 2), ROWS // 2, 0)
    far = split_shift(piece(3 * sign), 3, -3)
    half = split_shift(half, 4, 4)
    middle = split_shift(piece(-2 * sign), -2, 2)
    near = split_shift(piece(-sign), -1, 1)
    parts, far, middle = lax.optimization_barrier((parts, far, middle))

    share = jnp.sum(parts, axis=0).astype(BF16)[None]
    got = [share] + [y_shift(share, k) for k in range(1, 4)]
    got[3], half, near = lax.optimization_barrier((got[3], half, near))
    got.append(x_swap(jnp.concatenate(got)))
    image = turned_image(place, got)
    image, near, middle, far, half = lax.optimization_barrier((image, near, middle, far, half))
    other_first = hank_swap(jnp.concatenate([near, middle]))
    other_last = hank_swap(jnp.concatenate([far, half]))

    even = hank == 0
    ends = other_last[ROWS : ROWS + Q]
    fronts = [None] * NZ
    fronts[0], fronts[4] = own[:Q], jnp.where(even, half[:Q], ends)
    for k, mine, theirs in (
        (7, near[:Q], other_first[:Q]),
        (6, middle[:Q], other_first[ROWS : ROWS + Q]),
        (3, far[:Q], other_last[:Q]),
    ):
        fronts[k] = jnp.where(even, mine, theirs)
        fronts[NZ - k] = jnp.where(even, theirs, mine)
    given = core_swap(jnp.stack(fronts))
    later = jnp.concatenate([given[NZ - 1 :], given[: NZ - 1]], axis=0)
    edge = (((z - jnp.arange(NZ)) & (NZ - 1)) == NZ - 1)[:, None, None]
    ahead = jnp.where(core == 0, given, jnp.where(edge, jnp.zeros_like(later), later))

    def halo(k):
        return jnp.stack([jnp.where(even, ahead[k], ahead[NZ - k]), jnp.where(even, ahead[NZ - k], ahead[k])])

    forward = backward = image
    pieces = (
        [(near, 0), (other_first, 0)],
        [(middle, 0), (other_first, ROWS)],
        [(far, 0), (other_last, 0)],
    )
    running = None
    for step in range(1, 4):
        forward = z_shift(forward, 1)
        backward = z_shift(backward, -1)
        if step == 1:
            running = sketch_terms(place, ahead[:1], [(own, 0)], [image], None, None)
        turn = 0 if step == 3 else 1
        k = NZ - step if turn else step
        running = sketch_terms(place, halo(k), pieces[step - 1], [forward, backward], turn, running)
    top = z_shift(forward[: HALF_P // 2], 1)
    bottom = z_shift(backward[HALF_P // 2 :], -1)
    image = jnp.concatenate([top, bottom], axis=0)
    total = sketch_terms(place, ahead[4:5], [(half, 0), (other_last, ROWS)], [image], None, running, True)

    near_far = core_swap(total[1, 1])
    theirs = hank_swap((total[0, 1] + near_far).astype(BF16))
    factor = 1.0 / math.sqrt(ROWS * 16 * Q * REF)
    out = final_sketch(factor, place, 0, [total[0, 0], core_swap(total[1, 0])], None)
    return final_sketch(factor, place, 1, [theirs], out)[None]


def solution(mesh):
    in_specs = (P("tm", "chan"), P(), P())
    out_specs = P("chan", "tm", "hank", None)
    return jax.shard_map(
        per_device, mesh=mesh, in_specs=in_specs, out_specs=out_specs, check_vma=False
    )
```

```python
import functools
import math

import jax
import jax.numpy as jnp
from jax import lax
from jax.experimental import pallas as pl
from jax.experimental.pallas import tpu as pltpu
from jax.sharding import PartitionSpec as P

REF = 2048
BLK = 128
Q = 16
P_SIZE = 512
HALF_P = P_SIZE // 2
LAGS = Q // 2
ROWS = 512
NZ = 8
NCHAN = 8
CDEV = 64
SHARE = ROWS // NCHAN
F32 = jnp.float32
BF16 = jnp.bfloat16
VMEM = pltpu.VMEM
SMEM = pltpu.SMEM


def tm_shift(value, steps):
    first, last = max(0, -steps), min(16, 16 - steps)
    return lax.ppermute(value, "tm", [(i, i + steps) for i in range(first, last)])


def z_shift(value, steps):
    return lax.ppermute(value, "tm", [(i, (i + 2 * steps) % 16) for i in range(16)])


def split_shift(value, near, far):
    pairs = []
    for i in range(16):
        pairs.append((2 * i, 2 * ((i + 2 * near) % 16)))
        pairs.append((2 * i + 1, 2 * ((i + 2 * far) % 16) + 1))
    return lax.ppermute(value, ("tm", "hank"), pairs)


def core_swap(value):
    return lax.ppermute(value, "tm", [(i, i ^ 1) for i in range(16)])


def hank_swap(value):
    return lax.ppermute(value, "hank", [(0, 1), (1, 0)])


def y_shift(value, steps):
    return lax.ppermute(value, "chan", [(i, (i & 4) | ((i + steps) & 3)) for i in range(NCHAN)])


def x_swap(value):
    return lax.ppermute(value, "chan", [(i, i ^ 4) for i in range(NCHAN)])


def signs_kernel(place, blocks, seed, signs):
    first_block = place[0] * (1024 // BLK)
    start = seed[0] * 7919 + place[1] * HALF_P

    def step(q, used):
        local = blocks[q] - first_block
        owned = (local >= 0) & (local < 1024 // BLK)

        @pl.when(owned)
        def _():
            index = lax.broadcasted_iota(jnp.int32, (BLK, HALF_P), 0) * P_SIZE
            index = index + lax.broadcasted_iota(jnp.int32, (BLK, HALF_P), 1)
            for j in range(Q):
                mixed = index + (start + (j * REF + q * BLK) * P_SIZE)
                mixed = mixed ^ (mixed >> 15)
                mixed = mixed * 668265263
                mixed = mixed ^ (mixed >> 13)
                sign = jnp.where((mixed & 512) != 0, F32(-1), F32(1))
                signs[used, j * BLK : (j + 1) * BLK, :] = sign.astype(BF16)

        return used + owned.astype(jnp.int32)

    lax.fori_loop(0, REF // BLK, step, jnp.int32(0))


def images_kernel(place, blocks, records, behind, signs, out, staged, shifted):
    first_block = place[0] * (1024 // BLK)
    out[...] = jnp.zeros_like(out)

    def step(q, used):
        local = blocks[q] - first_block
        owned = (local >= 0) & (local < 1024 // BLK)

        @pl.when(owned)
        def _():
            cols = pl.ds(pl.multiple_of(local * BLK, BLK), BLK)
            staged[pl.ds(0, Q), :] = behind[:, cols].astype(F32)
            staged[pl.ds(Q, ROWS), :] = records[:, cols].astype(F32)
            for j in range(Q):
                shifted[:, j * BLK : (j + 1) * BLK] = staged[pl.ds(Q - j, ROWS), :].astype(BF16)
            out[...] += jnp.dot(shifted[...], signs[used], preferred_element_type=F32)

        return used + owned.astype(jnp.int32)

    lax.fori_loop(0, REF // BLK, step, jnp.int32(0))


def probe_signs(place, ref_blocks, probe_seed):
    return pl.pallas_call(
        signs_kernel,
        out_shape=jax.ShapeDtypeStruct((1024 // BLK, Q * BLK, HALF_P), BF16),
        in_specs=[pl.BlockSpec(memory_space=SMEM)] * 3,
        out_specs=pl.BlockSpec(memory_space=VMEM),
        compiler_params=pltpu.CompilerParams(vmem_limit_bytes=16 << 20),
        cost_estimate=pl.CostEstimate(flops=0, bytes_accessed=14 << 20, transcendentals=0),
        name="probe_signs",
    )(place, ref_blocks, probe_seed)


def partial_images(place, ref_blocks, records, behind, signs):
    return pl.pallas_call(
        images_kernel,
        out_shape=jax.ShapeDtypeStruct((ROWS, HALF_P), F32),
        in_specs=[pl.BlockSpec(memory_space=SMEM)] * 2 + [pl.BlockSpec(memory_space=VMEM)] * 3,
        out_specs=pl.BlockSpec(memory_space=VMEM),
        scratch_shapes=[pltpu.VMEM((ROWS + Q, BLK), F32), pltpu.VMEM((ROWS, Q * BLK), BF16)],
        compiler_params=pltpu.CompilerParams(vmem_limit_bytes=24 << 20),
        cost_estimate=pl.CostEstimate(flops=4 << 30, bytes_accessed=2 << 20, transcendentals=0),
        name="partial_images",
    )(place, ref_blocks, records, behind, signs)


def order_kernel(place, *refs):
    out, staged = refs[-2:]
    at = 0
    for ref in refs[:-2]:
        for entry in range(ref.shape[0]):
            k = ((place[0] & 4) ^ (at & 4)) | ((place[0] - at) & 3)
            staged[pl.ds(pl.multiple_of(k * SHARE, SHARE), SHARE), :] = ref[entry].astype(F32)
            at += 1
    out[...] = staged[...].T.astype(BF16)


def turned_image(place, parts):
    return pl.pallas_call(
        order_kernel,
        out_shape=jax.ShapeDtypeStruct((HALF_P, ROWS), BF16),
        in_specs=[pl.BlockSpec(memory_space=SMEM)] + [pl.BlockSpec(memory_space=VMEM)] * len(parts),
        out_specs=pl.BlockSpec(memory_space=VMEM),
        scratch_shapes=[pltpu.VMEM((ROWS, HALF_P), F32)],
        compiler_params=pltpu.CompilerParams(vmem_limit_bytes=8 << 20),
        cost_estimate=pl.CostEstimate(flops=0, bytes_accessed=3 << 20, transcendentals=0),
        name="turned_image",
    )(place, *parts)


def sketch_kernel(count, starts, turn, first, last, *refs):
    place, ahead = refs[:2]
    inputs = len(starts)
    rows, images = refs[2 : 2 + inputs], refs[2 + inputs : 2 + inputs + count]
    staged, total = refs[-2:]
    out = refs[-3]
    running = None if first else refs[2 + inputs + count]
    for n in range(count):
        if inputs == count:
            staged[pl.ds(0, ROWS), :] = rows[n][pl.ds(starts[n], ROWS), :].astype(F32)
        else:
            for m in range(2):
                at = pl.multiple_of((place[1] ^ m) * (ROWS // 2), ROWS // 2)
                staged[pl.ds(at, ROWS // 2), :] = rows[m][pl.ds(starts[m], ROWS // 2), :].astype(F32)
        staged[pl.ds(ROWS, Q), :] = ahead[n].astype(F32)
        image = images[n][...]
        if count == 2:
            image = jnp.where(place[1] == turn, image, images[1 - n][...])
        for m in range(LAGS):
            pair = [staged[pl.ds(2 * m + 1 + i, ROWS), :].astype(BF16) for i in range(2)]
            term = jnp.dot(image, jnp.concatenate(pair, axis=1), preferred_element_type=F32)
            at = slice(2 * m * BLK, (2 * m + 2) * BLK)
            goal = total if last or n < count - 1 else out
            if n == 0:
                goal[:, at] = term if first else running[:, at] + term
            else:
                goal[:, at] = total[:, at] + term
    if last:
        lane = lax.broadcasted_iota(jnp.int32, (HALF_P, BLK), 1)
        for m in range(LAGS):
            even = total[:, 2 * m * BLK : (2 * m + 1) * BLK]
            odd = total[:, (2 * m + 1) * BLK : (2 * m + 2) * BLK]
            low = jnp.where(lane < CDEV, even, pltpu.roll(odd, CDEV, 1))
            high = jnp.where(lane < CDEV, pltpu.roll(even, CDEV, 1), odd)
            side = (m // 4) ^ place[1]
            out[place[2], side, m % 4] = low
            out[1 - place[2], side, m % 4] = high


def sketch_terms(place, ahead, rows, images, turn, running, last=False):
    count, first = len(images), running is None
    starts = [start for _, start in rows]
    rows = [value for value, _ in rows]
    shape = (2, 2, 4, HALF_P, BLK) if last else (HALF_P, Q * BLK)
    args = [place, ahead, *rows, *images] + ([] if first else [running])
    return pl.pallas_call(
        functools.partial(sketch_kernel, count, starts, turn, first, last),
        out_shape=jax.ShapeDtypeStruct(shape, F32),
        in_specs=[pl.BlockSpec(memory_space=SMEM)] + [pl.BlockSpec(memory_space=VMEM)] * (len(args) - 1),
        out_specs=pl.BlockSpec(memory_space=VMEM),
        scratch_shapes=[pltpu.VMEM((ROWS + Q, BLK), F32), pltpu.VMEM((HALF_P, Q * BLK), F32)],
        compiler_params=pltpu.CompilerParams(vmem_limit_bytes=24 << 20),
        cost_estimate=pl.CostEstimate(flops=count << 30, bytes_accessed=2 << 20, transcendentals=0),
        name="sketch_terms",
    )(*args)


def final_kernel(factor, count, place, *refs):
    out = refs[-1]
    for m in range(LAGS // 2):
        value = refs[0][m].astype(F32)
        if count == 2:
            value = value + refs[1][m]
        value = (value * factor).T
        for i in range(2):
            out[:, 2 * m + i, :] = value[i * CDEV : (i + 1) * CDEV]


def final_sketch(factor, place, side, terms, out):
    whole = pl.BlockSpec((LAGS // 2, HALF_P, BLK), lambda i, place: (0, 0, 0))
    goal = pl.BlockSpec((CDEV, LAGS, HALF_P), lambda i, place: (0, 0, place[1] ^ side))
    args = list(terms)
    in_specs = [whole] * len(terms)
    aliases = {}
    if out is not None:
        args.append(out)
        in_specs.append(pl.BlockSpec(memory_space=pl.ANY))
        aliases = {len(terms) + 1: 0}
    return pl.pallas_call(
        functools.partial(final_kernel, factor, len(terms)),
        out_shape=jax.ShapeDtypeStruct((CDEV, LAGS, P_SIZE), F32),
        grid_spec=pltpu.PrefetchScalarGridSpec(
            num_scalar_prefetch=1, grid=(1,), in_specs=in_specs, out_specs=goal
        ),
        input_output_aliases=aliases,
        compiler_params=pltpu.CompilerParams(vmem_limit_bytes=16 << 20),
        name="final_sketch",
    )(place, *args)


def per_device(records, ref_blocks, probe_seed):
    tm = lax.axis_index("tm")
    z, core = tm >> 1, tm & 1
    hank = lax.axis_index("hank")
    chan = lax.axis_index("chan")
    place = jnp.stack([chan, hank, core]).astype(jnp.int32)

    behind = tm_shift(records[ROWS - Q :], 1)
    signs = probe_signs(place, ref_blocks, probe_seed)
    partial = partial_images(place, ref_blocks, records, behind, signs)

    partial, sent = lax.optimization_barrier((partial, records))
    parts = lax.all_to_all(partial.reshape(NCHAN, SHARE, HALF_P), "chan", 0, 0, tiled=True)
    sign = 1 - 2 * hank

    def piece(steps):
        return lax.dynamic_slice_in_dim(sent, ((z + steps) & (NZ - 1)) * BLK, BLK, 1)

    own = piece(0)
    half = lax.dynamic_slice_in_dim(piece(4), hank * (ROWS // 2), ROWS // 2, 0)
    far = split_shift(piece(3 * sign), 3, -3)
    half = split_shift(half, 4, 4)
    middle = split_shift(piece(-2 * sign), -2, 2)
    near = split_shift(piece(-sign), -1, 1)
    parts, near = lax.optimization_barrier((parts, near))

    share = jnp.sum(parts, axis=0).astype(BF16)[None]
    got = [share] + [y_shift(share, k) for k in range(1, 4)]
    got[3], middle, far = lax.optimization_barrier((got[3], middle, far))
    got.append(x_swap(jnp.concatenate(got)))
    image = turned_image(place, got)
    image, near, middle, far, half = lax.optimization_barrier((image, near, middle, far, half))
    other_first = hank_swap(jnp.concatenate([near, middle]))
    other_last = hank_swap(jnp.concatenate([far, half]))

    even = hank == 0
    ends = other_last[ROWS : ROWS + Q]
    fronts = [None] * NZ
    fronts[0], fronts[4] = own[:Q], jnp.where(even, half[:Q], ends)
    for k, mine, theirs in (
        (7, near[:Q], other_first[:Q]),
        (6, middle[:Q], other_first[ROWS : ROWS + Q]),
        (3, far[:Q], other_last[:Q]),
    ):
        fronts[k] = jnp.where(even, mine, theirs)
        fronts[NZ - k] = jnp.where(even, theirs, mine)
    given = core_swap(jnp.stack(fronts))
    later = jnp.concatenate([given[NZ - 1 :], given[: NZ - 1]], axis=0)
    edge = (((z - jnp.arange(NZ)) & (NZ - 1)) == NZ - 1)[:, None, None]
    ahead = jnp.where(core == 0, given, jnp.where(edge, jnp.zeros_like(later), later))

    def halo(k):
        return jnp.stack([jnp.where(even, ahead[k], ahead[NZ - k]), jnp.where(even, ahead[NZ - k], ahead[k])])

    forward = backward = image
    pieces = (
        [(near, 0), (other_first, 0)],
        [(middle, 0), (other_first, ROWS)],
        [(far, 0), (other_last, 0)],
    )
    running = None
    for step in range(1, 4):
        forward = z_shift(forward, 1)
        backward = z_shift(backward, -1)
        if step == 1:
            running = sketch_terms(place, ahead[:1], [(own, 0)], [image], None, None)
        turn = 0 if step == 3 else 1
        k = NZ - step if turn else step
        running = sketch_terms(place, halo(k), pieces[step - 1], [forward, backward], turn, running)
    top = z_shift(forward[: HALF_P // 2], 1)
    bottom = z_shift(backward[HALF_P // 2 :], -1)
    image = jnp.concatenate([top, bottom], axis=0)
    total = sketch_terms(place, ahead[4:5], [(half, 0), (other_last, ROWS)], [image], None, running, True)

    near_far = core_swap(total[1, 1])
    theirs = hank_swap((total[0, 1] + near_far).astype(BF16))
    factor = 1.0 / math.sqrt(ROWS * 16 * Q * REF)
    out = final_sketch(factor, place, 0, [total[0, 0], core_swap(total[1, 0])], None)
    return final_sketch(factor, place, 1, [theirs], out)[None]


def solution(mesh):
    in_specs = (P("tm", "chan"), P(), P())
    out_specs = P("chan", "tm", "hank", None)
    return jax.shard_map(
        per_device, mesh=mesh, in_specs=in_specs, out_specs=out_specs, check_vma=False
    )
```

```python
import functools
import math

import jax
import jax.numpy as jnp
from jax import lax
from jax.experimental import pallas as pl
from jax.experimental.pallas import tpu as pltpu
from jax.sharding import PartitionSpec as P

REF = 2048
BLK = 128
Q = 16
P_SIZE = 512
HALF_P = P_SIZE // 2
LAGS = Q // 2
ROWS = 512
NZ = 8
NCHAN = 8
CDEV = 64
SHARE = ROWS // NCHAN
F32 = jnp.float32
BF16 = jnp.bfloat16
VMEM = pltpu.VMEM
SMEM = pltpu.SMEM


def tm_shift(value, steps):
    first, last = max(0, -steps), min(16, 16 - steps)
    return lax.ppermute(value, "tm", [(i, i + steps) for i in range(first, last)])


def z_shift(value, steps):
    return lax.ppermute(value, "tm", [(i, (i + 2 * steps) % 16) for i in range(16)])


def split_shift(value, near, far):
    pairs = []
    for i in range(16):
        pairs.append((2 * i, 2 * ((i + 2 * near) % 16)))
        pairs.append((2 * i + 1, 2 * ((i + 2 * far) % 16) + 1))
    return lax.ppermute(value, ("tm", "hank"), pairs)


def core_swap(value):
    return lax.ppermute(value, "tm", [(i, i ^ 1) for i in range(16)])


def hank_swap(value):
    return lax.ppermute(value, "hank", [(0, 1), (1, 0)])


def chan_xor(value, bit):
    return lax.ppermute(value, "chan", [(i, i ^ bit) for i in range(NCHAN)])


def signs_kernel(place, blocks, seed, signs):
    first_block = place[0] * (1024 // BLK)
    start = seed[0] * 7919 + place[1] * HALF_P

    def step(q, used):
        local = blocks[q] - first_block
        owned = (local >= 0) & (local < 1024 // BLK)

        @pl.when(owned)
        def _():
            index = lax.broadcasted_iota(jnp.int32, (BLK, HALF_P), 0) * P_SIZE
            index = index + lax.broadcasted_iota(jnp.int32, (BLK, HALF_P), 1)
            for j in range(Q):
                mixed = index + (start + (j * REF + q * BLK) * P_SIZE)
                mixed = mixed ^ (mixed >> 15)
                mixed = mixed * 668265263
                mixed = mixed ^ (mixed >> 13)
                sign = jnp.where((mixed & 512) != 0, F32(-1), F32(1))
                signs[used, j * BLK : (j + 1) * BLK, :] = sign.astype(BF16)

        return used + owned.astype(jnp.int32)

    lax.fori_loop(0, REF // BLK, step, jnp.int32(0))


def images_kernel(place, blocks, records, behind, signs, out, staged, shifted):
    first_block = place[0] * (1024 // BLK)
    out[...] = jnp.zeros_like(out)

    def step(q, used):
        local = blocks[q] - first_block
        owned = (local >= 0) & (local < 1024 // BLK)

        @pl.when(owned)
        def _():
            cols = pl.ds(pl.multiple_of(local * BLK, BLK), BLK)
            staged[pl.ds(0, Q), :] = behind[:, cols].astype(F32)
            staged[pl.ds(Q, ROWS), :] = records[:, cols].astype(F32)
            for j in range(Q):
                shifted[:, j * BLK : (j + 1) * BLK] = staged[pl.ds(Q - j, ROWS), :].astype(BF16)
            out[...] += jnp.dot(shifted[...], signs[used], preferred_element_type=F32)

        return used + owned.astype(jnp.int32)

    lax.fori_loop(0, REF // BLK, step, jnp.int32(0))


def probe_signs(place, ref_blocks, probe_seed):
    return pl.pallas_call(
        signs_kernel,
        out_shape=jax.ShapeDtypeStruct((1024 // BLK, Q * BLK, HALF_P), BF16),
        in_specs=[pl.BlockSpec(memory_space=SMEM)] * 3,
        out_specs=pl.BlockSpec(memory_space=VMEM),
        compiler_params=pltpu.CompilerParams(vmem_limit_bytes=16 << 20),
        cost_estimate=pl.CostEstimate(flops=0, bytes_accessed=14 << 20, transcendentals=0),
        name="probe_signs",
    )(place, ref_blocks, probe_seed)


def partial_images(place, ref_blocks, records, behind, signs):
    return pl.pallas_call(
        images_kernel,
        out_shape=jax.ShapeDtypeStruct((ROWS, HALF_P), F32),
        in_specs=[pl.BlockSpec(memory_space=SMEM)] * 2 + [pl.BlockSpec(memory_space=VMEM)] * 3,
        out_specs=pl.BlockSpec(memory_space=VMEM),
        scratch_shapes=[pltpu.VMEM((ROWS + Q, BLK), F32), pltpu.VMEM((ROWS, Q * BLK), BF16)],
        compiler_params=pltpu.CompilerParams(vmem_limit_bytes=24 << 20),
        cost_estimate=pl.CostEstimate(flops=4 << 30, bytes_accessed=2 << 20, transcendentals=0),
        name="partial_images",
    )(place, ref_blocks, records, behind, signs)


def order_kernel(place, *refs):
    out, staged = refs[-2:]
    at = 0
    for ref in refs[:-2]:
        for entry in range(ref.shape[0]):
            k = place[0] ^ at
            staged[pl.ds(pl.multiple_of(k * SHARE, SHARE), SHARE), :] = ref[entry].astype(F32)
            at += 1
    out[...] = staged[...].T.astype(BF16)


def turned_image(place, parts):
    return pl.pallas_call(
        order_kernel,
        out_shape=jax.ShapeDtypeStruct((HALF_P, ROWS), BF16),
        in_specs=[pl.BlockSpec(memory_space=SMEM)] + [pl.BlockSpec(memory_space=VMEM)] * len(parts),
        out_specs=pl.BlockSpec(memory_space=VMEM),
        scratch_shapes=[pltpu.VMEM((ROWS, HALF_P), F32)],
        compiler_params=pltpu.CompilerParams(vmem_limit_bytes=8 << 20),
        cost_estimate=pl.CostEstimate(flops=0, bytes_accessed=3 << 20, transcendentals=0),
        name="turned_image",
    )(place, *parts)


def sketch_kernel(count, starts, turn, first, last, *refs):
    place, ahead = refs[:2]
    inputs = len(starts)
    rows, images = refs[2 : 2 + inputs], refs[2 + inputs : 2 + inputs + count]
    staged, total = refs[-2:]
    out = refs[-3]
    running = None if first else refs[2 + inputs + count]
    for n in range(count):
        if inputs == count:
            staged[pl.ds(0, ROWS), :] = rows[n][pl.ds(starts[n], ROWS), :].astype(F32)
        else:
            for m in range(2):
                at = pl.multiple_of((place[1] ^ m) * (ROWS // 2), ROWS // 2)
                staged[pl.ds(at, ROWS // 2), :] = rows[m][pl.ds(starts[m], ROWS // 2), :].astype(F32)
        staged[pl.ds(ROWS, Q), :] = ahead[n].astype(F32)
        image = images[n][...]
        if count == 2:
            image = jnp.where(place[1] == turn, image, images[1 - n][...])
        for m in range(LAGS):
            pair = [staged[pl.ds(2 * m + 1 + i, ROWS), :].astype(BF16) for i in range(2)]
            term = jnp.dot(image, jnp.concatenate(pair, axis=1), preferred_element_type=F32)
            at = slice(2 * m * BLK, (2 * m + 2) * BLK)
            goal = total if last or n < count - 1 else out
            if n == 0:
                goal[:, at] = term if first else running[:, at] + term
            else:
                goal[:, at] = total[:, at] + term
    if last:
        lane = lax.broadcasted_iota(jnp.int32, (HALF_P, BLK), 1)
        for m in range(LAGS):
            even = total[:, 2 * m * BLK : (2 * m + 1) * BLK]
            odd = total[:, (2 * m + 1) * BLK : (2 * m + 2) * BLK]
            low = jnp.where(lane < CDEV, even, pltpu.roll(odd, CDEV, 1))
            high = jnp.where(lane < CDEV, pltpu.roll(even, CDEV, 1), odd)
            side = (m // 4) ^ place[1]
            out[place[2], side, m % 4] = low
            out[1 - place[2], side, m % 4] = high


def sketch_terms(place, ahead, rows, images, turn, running, last=False):
    count, first = len(images), running is None
    starts = [start for _, start in rows]
    rows = [value for value, _ in rows]
    shape = (2, 2, 4, HALF_P, BLK) if last else (HALF_P, Q * BLK)
    args = [place, ahead, *rows, *images] + ([] if first else [running])
    return pl.pallas_call(
        functools.partial(sketch_kernel, count, starts, turn, first, last),
        out_shape=jax.ShapeDtypeStruct(shape, F32),
        in_specs=[pl.BlockSpec(memory_space=SMEM)] + [pl.BlockSpec(memory_space=VMEM)] * (len(args) - 1),
        out_specs=pl.BlockSpec(memory_space=VMEM),
        scratch_shapes=[pltpu.VMEM((ROWS + Q, BLK), F32), pltpu.VMEM((HALF_P, Q * BLK), F32)],
        compiler_params=pltpu.CompilerParams(vmem_limit_bytes=24 << 20),
        cost_estimate=pl.CostEstimate(flops=count << 30, bytes_accessed=2 << 20, transcendentals=0),
        name="sketch_terms",
    )(*args)


def final_kernel(factor, count, place, *refs):
    out = refs[-1]
    for m in range(LAGS // 2):
        value = refs[0][m].astype(F32)
        if count == 2:
            value = value + refs[1][m]
        value = (value * factor).T
        for i in range(2):
            out[:, 2 * m + i, :] = value[i * CDEV : (i + 1) * CDEV]


def final_sketch(factor, place, side, terms, out):
    whole = pl.BlockSpec((LAGS // 2, HALF_P, BLK), lambda i, place: (0, 0, 0))
    goal = pl.BlockSpec((CDEV, LAGS, HALF_P), lambda i, place: (0, 0, place[1] ^ side))
    args = list(terms)
    in_specs = [whole] * len(terms)
    aliases = {}
    if out is not None:
        args.append(out)
        in_specs.append(pl.BlockSpec(memory_space=pl.ANY))
        aliases = {len(terms) + 1: 0}
    return pl.pallas_call(
        functools.partial(final_kernel, factor, len(terms)),
        out_shape=jax.ShapeDtypeStruct((CDEV, LAGS, P_SIZE), F32),
        grid_spec=pltpu.PrefetchScalarGridSpec(
            num_scalar_prefetch=1, grid=(1,), in_specs=in_specs, out_specs=goal
        ),
        input_output_aliases=aliases,
        compiler_params=pltpu.CompilerParams(vmem_limit_bytes=16 << 20),
        name="final_sketch",
    )(place, *args)


def per_device(records, ref_blocks, probe_seed):
    tm = lax.axis_index("tm")
    z, core = tm >> 1, tm & 1
    hank = lax.axis_index("hank")
    chan = lax.axis_index("chan")
    place = jnp.stack([chan, hank, core]).astype(jnp.int32)

    behind = tm_shift(records[ROWS - Q :], 1)
    signs = probe_signs(place, ref_blocks, probe_seed)
    partial = partial_images(place, ref_blocks, records, behind, signs)

    partial, sent = lax.optimization_barrier((partial, records))
    parts = lax.all_to_all(partial.reshape(NCHAN, SHARE, HALF_P), "chan", 0, 0, tiled=True)
    sign = 1 - 2 * hank

    def piece(steps):
        return lax.dynamic_slice_in_dim(sent, ((z + steps) & (NZ - 1)) * BLK, BLK, 1)

    own = piece(0)
    half = lax.dynamic_slice_in_dim(piece(4), hank * (ROWS // 2), ROWS // 2, 0)
    far = split_shift(piece(3 * sign), 3, -3)
    half = split_shift(half, 4, 4)
    middle = split_shift(piece(-2 * sign), -2, 2)
    near = split_shift(piece(-sign), -1, 1)
    parts, near = lax.optimization_barrier((parts, near))

    share = jnp.sum(parts, axis=0).astype(BF16)[None]
    got = [share, chan_xor(share, 1)]
    got[1], middle, far = lax.optimization_barrier((got[1], middle, far))
    got.append(chan_xor(jnp.concatenate(got), 2))
    got[2], half = lax.optimization_barrier((got[2], half))
    got.append(chan_xor(jnp.concatenate(got), 4))
    image = turned_image(place, got)
    image, near, middle, far, half = lax.optimization_barrier((image, near, middle, far, half))
    other_first = hank_swap(jnp.concatenate([near, middle]))
    other_last = hank_swap(jnp.concatenate([far, half]))

    even = hank == 0
    ends = other_last[ROWS : ROWS + Q]
    fronts = [None] * NZ
    fronts[0], fronts[4] = own[:Q], jnp.where(even, half[:Q], ends)
    for k, mine, theirs in (
        (7, near[:Q], other_first[:Q]),
        (6, middle[:Q], other_first[ROWS : ROWS + Q]),
        (3, far[:Q], other_last[:Q]),
    ):
        fronts[k] = jnp.where(even, mine, theirs)
        fronts[NZ - k] = jnp.where(even, theirs, mine)
    given = core_swap(jnp.stack(fronts))
    later = jnp.concatenate([given[NZ - 1 :], given[: NZ - 1]], axis=0)
    edge = (((z - jnp.arange(NZ)) & (NZ - 1)) == NZ - 1)[:, None, None]
    ahead = jnp.where(core == 0, given, jnp.where(edge, jnp.zeros_like(later), later))

    def halo(k):
        return jnp.stack([jnp.where(even, ahead[k], ahead[NZ - k]), jnp.where(even, ahead[NZ - k], ahead[k])])

    forward = backward = image
    pieces = (
        [(near, 0), (other_first, 0)],
        [(middle, 0), (other_first, ROWS)],
        [(far, 0), (other_last, 0)],
    )
    running = None
    for step in range(1, 4):
        forward = z_shift(forward, 1)
        backward = z_shift(backward, -1)
        if step == 1:
            running = sketch_terms(place, ahead[:1], [(own, 0)], [image], None, None)
        turn = 0 if step == 3 else 1
        k = NZ - step if turn else step
        running = sketch_terms(place, halo(k), pieces[step - 1], [forward, backward], turn, running)
    top = z_shift(forward[: HALF_P // 2], 1)
    bottom = z_shift(backward[HALF_P // 2 :], -1)
    image = jnp.concatenate([top, bottom], axis=0)
    total = sketch_terms(place, ahead[4:5], [(half, 0), (other_last, ROWS)], [image], None, running, True)

    near_far = core_swap(total[1, 1])
    theirs = hank_swap((total[0, 1] + near_far).astype(BF16))
    factor = 1.0 / math.sqrt(ROWS * 16 * Q * REF)
    out = final_sketch(factor, place, 0, [total[0, 0], core_swap(total[1, 0])], None)
    return final_sketch(factor, place, 1, [theirs], out)[None]


def solution(mesh):
    in_specs = (P("tm", "chan"), P(), P())
    out_specs = P("chan", "tm", "hank", None)
    return jax.shard_map(
        per_device, mesh=mesh, in_specs=in_specs, out_specs=out_specs, check_vma=False
    )
```

```python
import functools
import math

import jax
import jax.numpy as jnp
from jax import lax
from jax.experimental import pallas as pl
from jax.experimental.pallas import tpu as pltpu
from jax.sharding import PartitionSpec as P

REF = 2048
BLK = 128
Q = 16
P_SIZE = 512
HALF_P = P_SIZE // 2
LAGS = Q // 2
ROWS = 512
NZ = 8
NCHAN = 8
CDEV = 64
SHARE = ROWS // NCHAN
F32 = jnp.float32
BF16 = jnp.bfloat16
VMEM = pltpu.VMEM
SMEM = pltpu.SMEM


def tm_shift(value, steps):
    first, last = max(0, -steps), min(16, 16 - steps)
    return lax.ppermute(value, "tm", [(i, i + steps) for i in range(first, last)])


def z_shift(value, steps):
    return lax.ppermute(value, "tm", [(i, (i + 2 * steps) % 16) for i in range(16)])


def split_shift(value, near, far):
    pairs = []
    for i in range(16):
        pairs.append((2 * i, 2 * ((i + 2 * near) % 16)))
        pairs.append((2 * i + 1, 2 * ((i + 2 * far) % 16) + 1))
    return lax.ppermute(value, ("tm", "hank"), pairs)


def core_swap(value):
    return lax.ppermute(value, "tm", [(i, i ^ 1) for i in range(16)])


def hank_swap(value):
    return lax.ppermute(value, "hank", [(0, 1), (1, 0)])


def y_shift(value, steps):
    return lax.ppermute(value, "chan", [(i, (i & 4) | ((i + steps) & 3)) for i in range(NCHAN)])


def x_swap(value):
    return lax.ppermute(value, "chan", [(i, i ^ 4) for i in range(NCHAN)])


def signs_kernel(place, blocks, seed, signs):
    first_block = place[0] * (1024 // BLK)
    start = seed[0] * 7919 + place[1] * HALF_P

    def step(q, used):
        local = blocks[q] - first_block
        owned = (local >= 0) & (local < 1024 // BLK)

        @pl.when(owned)
        def _():
            index = lax.broadcasted_iota(jnp.int32, (BLK, HALF_P), 0) * P_SIZE
            index = index + lax.broadcasted_iota(jnp.int32, (BLK, HALF_P), 1)
            for j in range(Q):
                mixed = index + (start + (j * REF + q * BLK) * P_SIZE)
                mixed = mixed ^ (mixed >> 15)
                mixed = mixed * 668265263
                mixed = mixed ^ (mixed >> 13)
                sign = jnp.where((mixed & 512) != 0, F32(-1), F32(1))
                signs[used, j * BLK : (j + 1) * BLK, :] = sign.astype(BF16)

        return used + owned.astype(jnp.int32)

    lax.fori_loop(0, REF // BLK, step, jnp.int32(0))


def images_kernel(place, blocks, records, behind, signs, out, staged, shifted):
    first_block = place[0] * (1024 // BLK)
    out[...] = jnp.zeros_like(out)

    def step(q, used):
        local = blocks[q] - first_block
        owned = (local >= 0) & (local < 1024 // BLK)

        @pl.when(owned)
        def _():
            cols = pl.ds(pl.multiple_of(local * BLK, BLK), BLK)
            staged[pl.ds(0, Q), :] = behind[:, cols].astype(F32)
            staged[pl.ds(Q, ROWS), :] = records[:, cols].astype(F32)
            for j in range(Q):
                shifted[:, j * BLK : (j + 1) * BLK] = staged[pl.ds(Q - j, ROWS), :].astype(BF16)
            out[...] += jnp.dot(shifted[...], signs[used], preferred_element_type=F32)

        return used + owned.astype(jnp.int32)

    lax.fori_loop(0, REF // BLK, step, jnp.int32(0))


def probe_signs(place, ref_blocks, probe_seed):
    return pl.pallas_call(
        signs_kernel,
        out_shape=jax.ShapeDtypeStruct((1024 // BLK, Q * BLK, HALF_P), BF16),
        in_specs=[pl.BlockSpec(memory_space=SMEM)] * 3,
        out_specs=pl.BlockSpec(memory_space=VMEM),
        compiler_params=pltpu.CompilerParams(vmem_limit_bytes=16 << 20),
        cost_estimate=pl.CostEstimate(flops=0, bytes_accessed=14 << 20, transcendentals=0),
        name="probe_signs",
    )(place, ref_blocks, probe_seed)


def partial_images(place, ref_blocks, records, behind, signs):
    return pl.pallas_call(
        images_kernel,
        out_shape=jax.ShapeDtypeStruct((ROWS, HALF_P), F32),
        in_specs=[pl.BlockSpec(memory_space=SMEM)] * 2 + [pl.BlockSpec(memory_space=VMEM)] * 3,
        out_specs=pl.BlockSpec(memory_space=VMEM),
        scratch_shapes=[pltpu.VMEM((ROWS + Q, BLK), F32), pltpu.VMEM((ROWS, Q * BLK), BF16)],
        compiler_params=pltpu.CompilerParams(vmem_limit_bytes=24 << 20),
        cost_estimate=pl.CostEstimate(flops=4 << 30, bytes_accessed=2 << 20, transcendentals=0),
        name="partial_images",
    )(place, ref_blocks, records, behind, signs)


def order_kernel(place, *refs):
    out, staged = refs[-2:]
    at = 0
    for ref in refs[:-2]:
        for entry in range(ref.shape[0]):
            k = ((place[0] & 4) ^ (at & 4)) | ((place[0] - at) & 3)
            staged[pl.ds(pl.multiple_of(k * SHARE, SHARE), SHARE), :] = ref[entry].astype(F32)
            at += 1
    out[...] = staged[...].T.astype(BF16)


def turned_image(place, parts):
    return pl.pallas_call(
        order_kernel,
        out_shape=jax.ShapeDtypeStruct((HALF_P, ROWS), BF16),
        in_specs=[pl.BlockSpec(memory_space=SMEM)] + [pl.BlockSpec(memory_space=VMEM)] * len(parts),
        out_specs=pl.BlockSpec(memory_space=VMEM),
        scratch_shapes=[pltpu.VMEM((ROWS, HALF_P), F32)],
        compiler_params=pltpu.CompilerParams(vmem_limit_bytes=8 << 20),
        cost_estimate=pl.CostEstimate(flops=0, bytes_accessed=3 << 20, transcendentals=0),
        name="turned_image",
    )(place, *parts)


def sketch_kernel(count, starts, turn, first, last, *refs):
    place, ahead = refs[:2]
    inputs = len(starts)
    rows, images = refs[2 : 2 + inputs], refs[2 + inputs : 2 + inputs + count]
    staged, total = refs[-2:]
    out = refs[-3]
    running = None if first else refs[2 + inputs + count]
    for n in range(count):
        if inputs == count:
            staged[pl.ds(0, ROWS), :] = rows[n][pl.ds(starts[n], ROWS), :].astype(F32)
        else:
            for m in range(2):
                at = pl.multiple_of((place[1] ^ m) * (ROWS // 2), ROWS // 2)
                staged[pl.ds(at, ROWS // 2), :] = rows[m][pl.ds(starts[m], ROWS // 2), :].astype(F32)
        staged[pl.ds(ROWS, Q), :] = ahead[n].astype(F32)
        image = images[n][...]
        if count == 2:
            image = jnp.where(place[1] == turn, image, images[1 - n][...])
        for m in range(LAGS):
            pair = [staged[pl.ds(2 * m + 1 + i, ROWS), :].astype(BF16) for i in range(2)]
            term = jnp.dot(image, jnp.concatenate(pair, axis=1), preferred_element_type=F32)
            at = slice(2 * m * BLK, (2 * m + 2) * BLK)
            goal = total if last or n < count - 1 else out
            if n == 0:
                goal[:, at] = term if first else running[:, at] + term
            else:
                goal[:, at] = total[:, at] + term
    if last:
        lane = lax.broadcasted_iota(jnp.int32, (HALF_P, BLK), 1)
        for m in range(LAGS):
            even = total[:, 2 * m * BLK : (2 * m + 1) * BLK]
            odd = total[:, (2 * m + 1) * BLK : (2 * m + 2) * BLK]
            low = jnp.where(lane < CDEV, even, pltpu.roll(odd, CDEV, 1))
            high = jnp.where(lane < CDEV, pltpu.roll(even, CDEV, 1), odd)
            side = (m // 4) ^ place[1]
            out[place[2], side, m % 4] = low
            out[1 - place[2], side, m % 4] = high


def sketch_terms(place, ahead, rows, images, turn, running, last=False):
    count, first = len(images), running is None
    starts = [start for _, start in rows]
    rows = [value for value, _ in rows]
    shape = (2, 2, 4, HALF_P, BLK) if last else (HALF_P, Q * BLK)
    args = [place, ahead, *rows, *images] + ([] if first else [running])
    return pl.pallas_call(
        functools.partial(sketch_kernel, count, starts, turn, first, last),
        out_shape=jax.ShapeDtypeStruct(shape, F32),
        in_specs=[pl.BlockSpec(memory_space=SMEM)] + [pl.BlockSpec(memory_space=VMEM)] * (len(args) - 1),
        out_specs=pl.BlockSpec(memory_space=VMEM),
        scratch_shapes=[pltpu.VMEM((ROWS + Q, BLK), F32), pltpu.VMEM((HALF_P, Q * BLK), F32)],
        compiler_params=pltpu.CompilerParams(vmem_limit_bytes=24 << 20),
        cost_estimate=pl.CostEstimate(flops=count << 30, bytes_accessed=2 << 20, transcendentals=0),
        name="sketch_terms",
    )(*args)


def final_kernel(factor, count, place, *refs):
    out = refs[-1]
    for m in range(LAGS // 2):
        value = refs[0][m].astype(F32)
        if count == 2:
            value = value + refs[1][m]
        value = (value * factor).T
        for i in range(2):
            out[:, 2 * m + i, :] = value[i * CDEV : (i + 1) * CDEV]


def final_sketch(factor, place, side, terms, out):
    whole = pl.BlockSpec((LAGS // 2, HALF_P, BLK), lambda i, place: (0, 0, 0))
    goal = pl.BlockSpec((CDEV, LAGS, HALF_P), lambda i, place: (0, 0, place[1] ^ side))
    args = list(terms)
    in_specs = [whole] * len(terms)
    aliases = {}
    if out is not None:
        args.append(out)
        in_specs.append(pl.BlockSpec(memory_space=pl.ANY))
        aliases = {len(terms) + 1: 0}
    return pl.pallas_call(
        functools.partial(final_kernel, factor, len(terms)),
        out_shape=jax.ShapeDtypeStruct((CDEV, LAGS, P_SIZE), F32),
        grid_spec=pltpu.PrefetchScalarGridSpec(
            num_scalar_prefetch=1, grid=(1,), in_specs=in_specs, out_specs=goal
        ),
        input_output_aliases=aliases,
        compiler_params=pltpu.CompilerParams(vmem_limit_bytes=16 << 20),
        name="final_sketch",
    )(place, *args)


def per_device(records, ref_blocks, probe_seed):
    tm = lax.axis_index("tm")
    z, core = tm >> 1, tm & 1
    hank = lax.axis_index("hank")
    chan = lax.axis_index("chan")
    place = jnp.stack([chan, hank, core]).astype(jnp.int32)

    behind = tm_shift(records[ROWS - Q :], 1)
    signs = probe_signs(place, ref_blocks, probe_seed)
    partial = partial_images(place, ref_blocks, records, behind, signs)

    partial, sent = lax.optimization_barrier((partial, records))
    parts = lax.all_to_all(partial.reshape(NCHAN, SHARE, HALF_P), "chan", 0, 0, tiled=True)
    sign = 1 - 2 * hank

    def piece(steps):
        return lax.dynamic_slice_in_dim(sent, ((z + steps) & (NZ - 1)) * BLK, BLK, 1)

    own = piece(0)
    half = lax.dynamic_slice_in_dim(piece(4), hank * (ROWS // 2), ROWS // 2, 0)
    far = split_shift(piece(3 * sign), 3, -3)
    half = split_shift(half, 4, 4)
    middle = split_shift(piece(-2 * sign), -2, 2)
    near = split_shift(piece(-sign), -1, 1)
    parts, half = lax.optimization_barrier((parts, half))

    share = jnp.sum(parts, axis=0).astype(BF16)[None]
    got = [share] + [y_shift(share, k) for k in range(1, 4)]
    got[3], middle, far = lax.optimization_barrier((got[3], middle, far))
    got.append(x_swap(jnp.concatenate(got)))
    image = turned_image(place, got)
    image, near, middle, far, half = lax.optimization_barrier((image, near, middle, far, half))
    other_first = hank_swap(jnp.concatenate([near, middle]))
    other_last = hank_swap(jnp.concatenate([far, half]))

    even = hank == 0
    ends = other_last[ROWS : ROWS + Q]
    fronts = [None] * NZ
    fronts[0], fronts[4] = own[:Q], jnp.where(even, half[:Q], ends)
    for k, mine, theirs in (
        (7, near[:Q], other_first[:Q]),
        (6, middle[:Q], other_first[ROWS : ROWS + Q]),
        (3, far[:Q], other_last[:Q]),
    ):
        fronts[k] = jnp.where(even, mine, theirs)
        fronts[NZ - k] = jnp.where(even, theirs, mine)
    given = core_swap(jnp.stack(fronts))
    later = jnp.concatenate([given[NZ - 1 :], given[: NZ - 1]], axis=0)
    edge = (((z - jnp.arange(NZ)) & (NZ - 1)) == NZ - 1)[:, None, None]
    ahead = jnp.where(core == 0, given, jnp.where(edge, jnp.zeros_like(later), later))

    def halo(k):
        return jnp.stack([jnp.where(even, ahead[k], ahead[NZ - k]), jnp.where(even, ahead[NZ - k], ahead[k])])

    forward = backward = image
    pieces = (
        [(near, 0), (other_first, 0)],
        [(middle, 0), (other_first, ROWS)],
        [(far, 0), (other_last, 0)],
    )
    running = None
    for step in range(1, 4):
        forward = z_shift(forward, 1)
        backward = z_shift(backward, -1)
        if step == 1:
            running = sketch_terms(place, ahead[:1], [(own, 0)], [image], None, None)
        turn = 0 if step == 3 else 1
        k = NZ - step if turn else step
        running = sketch_terms(place, halo(k), pieces[step - 1], [forward, backward], turn, running)
    top = z_shift(forward[: HALF_P // 2], 1)
    bottom = z_shift(backward[HALF_P // 2 :], -1)
    image = jnp.concatenate([top, bottom], axis=0)
    total = sketch_terms(place, ahead[4:5], [(half, 0), (other_last, ROWS)], [image], None, running, True)

    near_far = core_swap(total[1, 1])
    theirs = hank_swap((total[0, 1] + near_far).astype(BF16))
    factor = 1.0 / math.sqrt(ROWS * 16 * Q * REF)
    out = final_sketch(factor, place, 0, [total[0, 0], core_swap(total[1, 0])], None)
    return final_sketch(factor, place, 1, [theirs], out)[None]


def solution(mesh):
    in_specs = (P("tm", "chan"), P(), P())
    out_specs = P("chan", "tm", "hank", None)
    return jax.shard_map(
        per_device, mesh=mesh, in_specs=in_specs, out_specs=out_specs, check_vma=False
    )
```
